512 devices in a mesh: rows: 128 (over y, z, core), grp: 4 (over x).
Axes of the slice: x: 4, y: 4, z: 16, core: 2. Of those that a mesh axis runs over, the one named last changes fastest.
Arguments:
- features: float32 [131072, 128], P(('rows', 'grp'))
- key_ids: int32 [131072], P(('rows', 'grp')), may hold values from 0 to 23, as said below
- owner: int32 [24], replicated, may hold values from 0 to 23, each once
Outputs:
- covariance: float32 [3072, 128], P(('rows', 'grp'))
The draws below stay inside these ranges and needn't reach their ends.
Inputs may be any that keep to these rules, and one draw needn't show every extreme that they name: `key_ids`: every key is the key of at least 2 rows.
All inputs are finite; a program needn't handle non-finite values.
Results may differ from the reference program's by a relative error of at most 0.0003.
Values sent between devices are 32-bit elements; how exact they have to be, the bound alone decides.
No kernel may reach another device: no remote copies, remote signals or barrier semaphores. Data moves between devices by JAX's collectives and lax.ppermute only.
A program may use at most 64 MiB of HBM per device.

```python
import math
import jax
import jax.numpy as jnp
from jax import lax

F = 128
KEYS = 24
ROWS = 131072


def draw_key_ids(key, part):
    first, second, third = jax.random.split(jax.random.fold_in(key, 11), 3)
    left = jax.random.randint(first, (ROWS,), 0, KEYS)
    right = jax.random.randint(second, (ROWS,), 0, KEYS)
    ranked = left * right // KEYS
    order = jax.random.permutation(third, KEYS)
    chosen = order[ranked]
    position = jnp.arange(ROWS, dtype=jnp.int32)
    chosen = jnp.where(position < 2 * KEYS, position % KEYS, chosen)
    return chosen.astype(jnp.int32)


def draw_features(key, part):
    first, second = jax.random.split(jax.random.fold_in(key, 23), 2)
    offsets = jax.random.uniform(second, (1, F), jnp.float32, -3.0, 3.0)
    values = jax.random.normal(first, (ROWS, F), jnp.float32)
    return (values + offsets).astype(jnp.float32)


def setup_inputs(seed: int = 0) -> dict:
    arg_keys = jax.random.split(jax.random.key(seed), 4)
    features = draw_features(jax.random.fold_in(arg_keys[3], 71), 0)
    key_ids = draw_key_ids(jax.random.fold_in(arg_keys[3], 71), 0)
    owner = jax.random.permutation(arg_keys[2], KEYS).astype(jnp.int32)
    return dict(features=features, key_ids=key_ids, owner=owner)


def reference(features, key_ids, owner):
    slot = owner[key_ids].astype(jnp.int32)
    count = jax.ops.segment_sum(jnp.ones((ROWS,), jnp.float32), slot, KEYS)
    total = jax.ops.segment_sum(features, slot, KEYS)
    block = math.gcd(ROWS, 1024)
    steps = ROWS // block

    def accumulate(acc, index):
        start = (index * block).astype(jnp.int32)
        piece = lax.dynamic_slice_in_dim(features, start, block, 0)
        labels = lax.dynamic_slice_in_dim(slot, start, block, 0)
        outer = piece[:, :, None] * piece[:, None, :]
        return acc + jax.ops.segment_sum(outer, labels, KEYS), None

    gram, _ = lax.scan(accumulate, jnp.zeros((KEYS, F, F), jnp.float32), jnp.arange(steps, dtype=jnp.int32))
    centred = gram - total[:, :, None] * total[:, None, :] / count[:, None, None]
    result = centred / (count - 1.0)[:, None, None]
    return result.reshape(KEYS * F, F)
```

```python
import jax
import jax.numpy as jnp
from jax import lax
from jax.experimental import pallas as pl
from jax.experimental.pallas import tpu as pltpu
from jax.sharding import Mesh
from jax.sharding import PartitionSpec as P

Y, Z, C, X = "y", "z", "c", "x"
ALL = (Y, Z, C, X)
F = 128
KEYS = 24
NY, NZ, NX = 4, 16, 4
OWN = 6
PACK = 264
MSG = 104
VMEM = pl.BlockSpec(memory_space=pltpu.VMEM)
SMEM = pl.BlockSpec(memory_space=pltpu.SMEM)
PARAMS = pltpu.CompilerParams(vmem_limit_bytes=16 * 1024 * 1024)


def pack_kernel(owner_ref, features_ref, keys_ref, out_ref):
    keys = keys_ref[...]
    slot = jnp.zeros(keys.shape, jnp.float32)
    for key in range(KEYS):
        slot = jnp.where(keys == key, owner_ref[key].astype(jnp.float32), slot)
    rows = features_ref.shape[0]
    out_ref[0:rows, :] = features_ref[...]
    out_ref[rows:, :] = jnp.concatenate([slot, jnp.zeros((6, F), jnp.float32)], axis=0)


def gram_kernel(rows_ref, out_ref):
    c = lax.axis_index(C)
    rows = PACK - 8
    feats = jnp.concatenate([rows_ref[0:rows, :], rows_ref[PACK : PACK + rows, :]], axis=0)
    first, second = rows_ref[rows:PACK, :], rows_ref[PACK + rows :, :]
    slot = jnp.concatenate([first[0:1], first[1:2], second[0:1], second[1:2]], axis=1)
    hi = feats.astype(jnp.bfloat16)
    lo = (feats - hi.astype(jnp.float32)).astype(jnp.bfloat16)
    both = jnp.concatenate([hi, lo], axis=1)

    m = NX * OWN * 8
    index = lax.broadcasted_iota(jnp.int32, (m, 1), 0)
    line = 48 * (index & 7) + 24 * c + (index >> 3)
    lane = lax.broadcasted_iota(jnp.int32, (m, F), 1)
    select = (lane == (line & 127)).astype(jnp.float32).astype(jnp.bfloat16)
    nt = (((1,), (1,)), ((), ()))
    nn = (((1,), (0,)), ((), ()))
    left_hi = lax.dot_general(select, hi, nt, preferred_element_type=jnp.float32)
    left_lo = lax.dot_general(select, lo, nt, preferred_element_type=jnp.float32)
    relative = slot - (line >> 7).astype(jnp.float32)

    index = lax.broadcasted_iota(jnp.int32, (32, 1), 0)
    wanted = jnp.where((index & 7) < 6, 6 * (index >> 3) + (index & 7), -1).astype(jnp.float32)
    onehot = (slot == wanted).astype(jnp.float32).astype(jnp.bfloat16)
    total = lax.dot_general(onehot, both, nn, preferred_element_type=jnp.float32)
    total = total[:, :F] + total[:, F:]
    label = lax.broadcasted_iota(jnp.int32, (F, 1), 0).astype(jnp.float32)
    every = (slot == label).astype(jnp.float32).astype(jnp.bfloat16)
    ones = jnp.ones((16, slot.shape[1]), jnp.bfloat16)
    count = lax.dot_general(ones, every, nt, preferred_element_type=jnp.float32)[0:8]
    sub = lax.broadcasted_iota(jnp.int32, (8, F), 0)
    for y in range(NY):
        tile = jnp.where(sub < 6, total[8 * y : 8 * y + 8], count)
        for x in range(NX):
            out_ref[y * NX + x, 96:104, :] = tile

    for group in range(8):
        y, half = group // 2, group % 2
        mine = relative == float(3 * group)
        a = jnp.where(mine, left_hi, 0.0).astype(jnp.bfloat16)
        b = jnp.where(mine, left_lo, 0.0).astype(jnp.bfloat16)
        wide = lax.dot_general(a, both, nn, preferred_element_type=jnp.float32)
        gram = wide[:, :F] + (
            wide[:, F:] + lax.dot_general(b, hi, nn, preferred_element_type=jnp.float32)
        )
        for x in range(NX):
            for i in range(OWN):
                at = (x * OWN + i) * 8
                out_ref[y * NX + x, i * 16 + half * 8 : i * 16 + half * 8 + 8, :] = gram[at : at + 8]


def relay_kernel(in_ref, out_ref):
    y, c, x = lax.axis_index(Y), lax.axis_index(C), lax.axis_index(X)
    total = jnp.sum(in_ref[...], axis=0)
    sums, counts = total[96:104], total[102:103]
    z = lax.broadcasted_iota(jnp.int32, (NZ, 1), 0)
    lane = lax.broadcasted_iota(jnp.int32, (NZ, F), 1)
    line = 48 * z + 24 * c + 6 * x
    head, tail = line >> 7, (line + 5) >> 7

    def pick(which):
        out = jnp.zeros((NZ, F), jnp.float32)
        for j in range(6):
            out = jnp.where(which == j, sums[j : j + 1], out)
        return out

    def number(which):
        return jnp.sum(jnp.where(lane == which + 6 * y, counts, 0.0), axis=1, keepdims=True)

    for i in range(OWN):
        part = total[16 * i : 16 * i + 16]
        if i == 1:
            part = jnp.where(lane == (line & 127), number(head), part)
        if i == 5:
            part = jnp.where(lane == ((line + 4) & 127), number(tail), part)
        out_ref[:, i, :] = part
    out_ref[:, 6, :] = pick(head)
    out_ref[:, 7, :] = pick(tail)


def final_kernel(in_ref, out_ref):
    z, c, x = lax.axis_index(Z), lax.axis_index(C), lax.axis_index(X)
    total = jnp.sum(in_ref[...], axis=0)
    start = (48 * z + 24 * c + 6 * x) & 127
    lane = lax.broadcasted_iota(jnp.int32, (1, F), 1)

    def entry(row, column):
        return jnp.sum(jnp.where(lane == column, total[row : row + 1], 0.0), axis=1, keepdims=True)

    fifth = (start + 4) & 127
    count_head, count_tail = entry(1, start), entry(5, fifth)
    fix_head, fix_tail = entry(0, start + 1), entry(4, fifth + 1)
    sub = lax.broadcasted_iota(jnp.int32, (8, 1), 0)
    wide = lax.broadcasted_iota(jnp.int32, (8, F), 1)
    gram = jnp.where((sub == 1) & (wide == start), fix_head, total)
    gram = jnp.where((sub == 5) & (wide == fifth), fix_tail, gram)
    in_head = start + sub < F
    slot_total = jnp.where(in_head, total[6:7], total[7:8])
    count = jnp.where(in_head, count_head, count_tail)
    own = jnp.sum(jnp.where(wide == ((start + sub) & 127), slot_total, 0.0), axis=1, keepdims=True)
    result = (gram - own * slot_total / count) / (count - 1.0)
    out_ref[...] = result[0:OWN]


def local(features, key_ids, owner):
    packed = pl.pallas_call(
        pack_kernel,
        out_shape=jax.ShapeDtypeStruct((PACK, F), jnp.float32),
        in_specs=[SMEM, VMEM, VMEM],
        out_specs=VMEM,
        compiler_params=PARAMS,
        name="pack",
    )(owner, features, key_ids.reshape(2, F))
    pair = lax.all_gather(packed, C, tiled=True)
    partial = pl.pallas_call(
        gram_kernel,
        out_shape=jax.ShapeDtypeStruct((NY * NX, MSG, F), jnp.float32),
        in_specs=[VMEM],
        out_specs=VMEM,
        compiler_params=PARAMS,
        name="gram",
    )(pair)
    near = lax.all_to_all(partial, (Y, X), 0, 0, tiled=True)
    relayed = pl.pallas_call(
        relay_kernel,
        out_shape=jax.ShapeDtypeStruct((NZ, 8, F), jnp.float32),
        in_specs=[VMEM],
        out_specs=VMEM,
        compiler_params=PARAMS,
        name="relay",
    )(near)
    far = lax.all_to_all(relayed, Z, 0, 0, tiled=True)
    return pl.pallas_call(
        final_kernel,
        out_shape=jax.ShapeDtypeStruct((OWN, F), jnp.float32),
        in_specs=[VMEM],
        out_specs=VMEM,
        compiler_params=PARAMS,
        name="finish",
    )(far)


def solution(mesh):
    torus = Mesh(mesh.devices.reshape(NY, NZ, 2, NX), ALL)
    in_specs = (P(ALL, None), P(ALL), P())
    return jax.shard_map(local, mesh=torus, in_specs=in_specs, out_specs=P(ALL, None), check_vma=False)
```

```python
import jax
import jax.numpy as jnp
from jax import lax
from jax.experimental import pallas as pl
from jax.experimental.pallas import tpu as pltpu
from jax.sharding import Mesh
from jax.sharding import PartitionSpec as P

Y, Z, C, X = "y", "z", "c", "x"
ALL = (Y, Z, C, X)
F = 128
KEYS = 24
NY, NZ, NX = 4, 16, 4
OWN = 6
PACK = 264
MSG = 104
VMEM = pl.BlockSpec(memory_space=pltpu.VMEM)
HBM = pl.BlockSpec(memory_space=pltpu.HBM)
Y0, Z0, X0 = 2, 10, 2
NEAR = [(i + X0) % NX * NY + (j + Y0) % NY for i in range(NX) for j in range(NY)]
FAR = [(k + Z0) % NZ for k in range(NZ)]
PARAMS = pltpu.CompilerParams(vmem_limit_bytes=16 * 1024 * 1024)


def pack_kernel(owner_ref, features_ref, keys_ref, out_ref, owner_buf, keys_buf, sems):
    rows = features_ref.shape[0]
    copies = [
        pltpu.make_async_copy(owner_ref, owner_buf, sems.at[0]),
        pltpu.make_async_copy(keys_ref, keys_buf, sems.at[1]),
        pltpu.make_async_copy(features_ref, out_ref.at[0:rows, :], sems.at[2]),
    ]
    for copy in copies:
        copy.start()
    copies[0].wait()
    copies[1].wait()
    keys = keys_buf[...]
    slot = jnp.zeros(keys.shape, jnp.float32)
    for key in range(KEYS):
        slot = jnp.where(keys == key, owner_buf[key].astype(jnp.float32), slot)
    out_ref[rows:, :] = jnp.concatenate([slot, jnp.zeros((6, F), jnp.float32)], axis=0)
    copies[2].wait()


def gram_kernel(rows_ref, out_ref):
    c = lax.axis_index(C)
    rows = PACK - 8
    feats = jnp.concatenate([rows_ref[0:rows, :], rows_ref[PACK : PACK + rows, :]], axis=0)
    first, second = rows_ref[rows:PACK, :], rows_ref[PACK + rows :, :]
    slot = jnp.concatenate([first[0:1], first[1:2], second[0:1], second[1:2]], axis=1)
    hi = feats.astype(jnp.bfloat16)
    lo = (feats - hi.astype(jnp.float32)).astype(jnp.bfloat16)
    both = jnp.concatenate([hi, lo], axis=1)

    m = NX * OWN * 8
    index = lax.broadcasted_iota(jnp.int32, (m, 1), 0)
    line = 48 * (index & 7) + 24 * c + (index >> 3)
    lane = lax.broadcasted_iota(jnp.int32, (m, F), 1)
    select = (lane == (line & 127)).astype(jnp.float32).astype(jnp.bfloat16)
    nt = (((1,), (1,)), ((), ()))
    nn = (((1,), (0,)), ((), ()))
    left_hi = lax.dot_general(select, hi, nt, preferred_element_type=jnp.float32)
    left_lo = lax.dot_general(select, lo, nt, preferred_element_type=jnp.float32)
    relative = slot - (line >> 7).astype(jnp.float32)

    index = lax.broadcasted_iota(jnp.int32, (32, 1), 0)
    wanted = jnp.where((index & 7) < 6, 6 * (index >> 3) + (index & 7), -1).astype(jnp.float32)
    onehot = (slot == wanted).astype(jnp.float32).astype(jnp.bfloat16)
    total = lax.dot_general(onehot, both, nn, preferred_element_type=jnp.float32)
    total = total[:, :F] + total[:, F:]
    label = lax.broadcasted_iota(jnp.int32, (F, 1), 0).astype(jnp.float32)
    every = (slot == label).astype(jnp.float32).astype(jnp.bfloat16)
    ones = jnp.ones((16, slot.shape[1]), jnp.bfloat16)
    count = lax.dot_general(ones, every, nt, preferred_element_type=jnp.float32)[0:8]
    sub = lax.broadcasted_iota(jnp.int32, (8, F), 0)
    for y in range(NY):
        tile = jnp.where(sub < 6, total[8 * y : 8 * y + 8], count)
        for x in range(NX):
            out_ref[NEAR.index(x * NY + y), 96:104, :] = tile

    for group in range(8):
        y, half = group // 2, group % 2
        mine = relative == float(3 * group)
        a = jnp.where(mine, left_hi, 0.0).astype(jnp.bfloat16)
        b = jnp.where(mine, left_lo, 0.0).astype(jnp.bfloat16)
        wide = lax.dot_general(a, both, nn, preferred_element_type=jnp.float32)
        gram = wide[:, :F] + (
            wide[:, F:] + lax.dot_general(b, hi, nn, preferred_element_type=jnp.float32)
        )
        for x in range(NX):
            for i in range(OWN):
                at = (x * OWN + i) * 8
                out_ref[NEAR.index(x * NY + y), i * 16 + half * 8 : i * 16 + half * 8 + 8, :] = gram[at : at + 8]


def relay_kernel(in_ref, out_ref):
    y, c, x = lax.axis_index(Y), lax.axis_index(C), lax.axis_index(X)
    total = jnp.sum(in_ref[...], axis=0)
    sums, counts = total[96:104], total[102:103]
    z = lax.broadcasted_iota(jnp.int32, (NZ, 1), 0)
    lane = lax.broadcasted_iota(jnp.int32, (NZ, F), 1)
    line = 48 * z + 24 * c + 6 * x
    head, tail = line >> 7, (line + 5) >> 7

    def pick(which):
        out = jnp.zeros((NZ, F), jnp.float32)
        for j in range(6):
            out = jnp.where(which == j, sums[j : j + 1], out)
        return out

    def number(which):
        return jnp.sum(jnp.where(lane == which + 6 * y, counts, 0.0), axis=1, keepdims=True)

    def put(i, part):
        out_ref[0 : NZ - Z0, i, :] = part[Z0:]
        out_ref[NZ - Z0 :, i, :] = part[:Z0]

    for i in range(OWN):
        part = total[16 * i : 16 * i + 16]
        if i == 1:
            part = jnp.where(lane == (line & 127), number(head), part)
        if i == 5:
            part = jnp.where(lane == ((line + 4) & 127), number(tail), part)
        put(i, part)
    put(6, pick(head))
    put(7, pick(tail))


def final_kernel(in_ref, out_ref):
    z, c, x = lax.axis_index(Z), lax.axis_index(C), lax.axis_index(X)
    total = jnp.sum(in_ref[...], axis=0)
    start = (48 * z + 24 * c + 6 * x) & 127
    lane = lax.broadcasted_iota(jnp.int32, (1, F), 1)

    def entry(row, column):
        return jnp.sum(jnp.where(lane == column, total[row : row + 1], 0.0), axis=1, keepdims=True)

    fifth = (start + 4) & 127
    count_head, count_tail = entry(1, start), entry(5, fifth)
    fix_head, fix_tail = entry(0, start + 1), entry(4, fifth + 1)
    sub = lax.broadcasted_iota(jnp.int32, (8, 1), 0)
    wide = lax.broadcasted_iota(jnp.int32, (8, F), 1)
    gram = jnp.where((sub == 1) & (wide == start), fix_head, total)
    gram = jnp.where((sub == 5) & (wide == fifth), fix_tail, gram)
    in_head = start + sub < F
    slot_total = jnp.where(in_head, total[6:7], total[7:8])
    count = jnp.where(in_head, count_head, count_tail)
    own = jnp.sum(jnp.where(wide == ((start + sub) & 127), slot_total, 0.0), axis=1, keepdims=True)
    result = (gram - own * slot_total / count) / (count - 1.0)
    out_ref[...] = result[0:OWN]


def local(features, key_ids, owner):
    packed = pl.pallas_call(
        pack_kernel,
        out_shape=jax.ShapeDtypeStruct((PACK, F), jnp.float32),
        in_specs=[HBM, HBM, HBM],
        out_specs=VMEM,
        scratch_shapes=[
            pltpu.SMEM((KEYS,), jnp.int32),
            pltpu.VMEM((2, F), jnp.int32),
            pltpu.SemaphoreType.DMA((3,)),
        ],
        compiler_params=PARAMS,
        name="pack",
    )(*(pltpu.with_memory_space_constraint(v, pltpu.HBM) for v in (owner, features, key_ids.reshape(2, F))))
    pair = lax.all_gather(packed, C, tiled=True)
    partial = pl.pallas_call(
        gram_kernel,
        out_shape=jax.ShapeDtypeStruct((NY * NX, MSG, F), jnp.float32),
        in_specs=[VMEM],
        out_specs=VMEM,
        compiler_params=PARAMS,
        name="gram",
    )(pair)
    near = lax.all_to_all(partial, (X, Y), 0, 0, axis_index_groups=[NEAR], tiled=True)
    relayed = pl.pallas_call(
        relay_kernel,
        out_shape=jax.ShapeDtypeStruct((NZ, 8, F), jnp.float32),
        in_specs=[VMEM],
        out_specs=VMEM,
        compiler_params=PARAMS,
        name="relay",
    )(near)
    far = lax.all_to_all(relayed, Z, 0, 0, axis_index_groups=[FAR], tiled=True)
    return pl.pallas_call(
        final_kernel,
        out_shape=jax.ShapeDtypeStruct((OWN, F), jnp.float32),
        in_specs=[VMEM],
        out_specs=VMEM,
        compiler_params=PARAMS,
        name="finish",
    )(far)


def solution(mesh):
    torus = Mesh(mesh.devices.reshape(NY, NZ, 2, NX), ALL)
    in_specs = (P(ALL, None), P(ALL), P())
    return jax.shard_map(local, mesh=torus, in_specs=in_specs, out_specs=P(ALL, None), check_vma=False)
```

```python
import jax
import jax.numpy as jnp
from jax import lax
from jax.experimental import pallas as pl
from jax.experimental.pallas import tpu as pltpu
from jax.sharding import Mesh
from jax.sharding import PartitionSpec as P

Y, Z, C, X = "y", "z", "c", "x"
ALL = (Y, Z, C, X)
F = 128
KEYS = 24
NY, NZ, NX = 4, 16, 4
OWN = 6
PACK = 264
MSG = 56
VMEM = pl.BlockSpec(memory_space=pltpu.VMEM)
HBM = pl.BlockSpec(memory_space=pltpu.HBM)
Y0, Z0, X0 = 2, 5, 2
NEAR = [(i + X0) % NX * NY + (j + Y0) % NY for i in range(NX) for j in range(NY)]
FAR = [[(2 * (k + Z0) + odd) % NZ for k in range(8)] for odd in range(2)]
PAIRS = [[4 * k + j for j in range(4)] for k in range(8)]
PARAMS = pltpu.CompilerParams(vmem_limit_bytes=16 * 1024 * 1024)


def pack_kernel(owner_ref, features_ref, keys_ref, out_ref, owner_buf, keys_buf, sems):
    rows = features_ref.shape[0]
    copies = [
        pltpu.make_async_copy(owner_ref, owner_buf, sems.at[0]),
        pltpu.make_async_copy(keys_ref, keys_buf, sems.at[1]),
        pltpu.make_async_copy(features_ref, out_ref.at[0:rows, :], sems.at[2]),
    ]
    for copy in copies:
        copy.start()
    copies[0].wait()
    copies[1].wait()
    keys = keys_buf[...]
    slot = jnp.zeros(keys.shape, jnp.float32)
    for key in range(KEYS):
        slot = jnp.where(keys == key, owner_buf[key].astype(jnp.float32), slot)
    out_ref[rows:, :] = jnp.concatenate([slot, jnp.zeros((6, F), jnp.float32)], axis=0)
    copies[2].wait()


def gram_kernel(rows_ref, out_ref):
    c, z = lax.axis_index(C), lax.axis_index(Z)
    rows = PACK - 8
    starts = range(0, 4 * PACK, PACK)
    feats = jnp.concatenate([rows_ref[at : at + rows, :] for at in starts], axis=0)
    slots = [rows_ref[at + rows : at + PACK, :] for at in starts]
    slot = jnp.concatenate([s[j : j + 1] for s in slots for j in range(2)], axis=1)
    hi = feats.astype(jnp.bfloat16)
    lo = (feats - hi.astype(jnp.float32)).astype(jnp.bfloat16)
    both = jnp.concatenate([hi, lo], axis=1)

    m = NX * OWN * 8
    index = lax.broadcasted_iota(jnp.int32, (m, 1), 0)
    line = 96 * (index & 7) + 48 * (z & 1) + 24 * c + (index >> 3)
    lane = lax.broadcasted_iota(jnp.int32, (m, F), 1)
    select = (lane == (line & 127)).astype(jnp.float32).astype(jnp.bfloat16)
    nt = (((1,), (1,)), ((), ()))
    nn = (((1,), (0,)), ((), ()))
    left_hi = lax.dot_general(select, hi, nt, preferred_element_type=jnp.float32)
    left_lo = lax.dot_general(select, lo, nt, preferred_element_type=jnp.float32)
    relative = slot - (line >> 7).astype(jnp.float32)

    index = lax.broadcasted_iota(jnp.int32, (32, 1), 0)
    wanted = jnp.where((index & 7) < 6, 6 * (index >> 3) + (index & 7), -1).astype(jnp.float32)
    onehot = (slot == wanted).astype(jnp.float32).astype(jnp.bfloat16)
    total = lax.dot_general(onehot, both, nn, preferred_element_type=jnp.float32)
    total = total[:, :F] + total[:, F:]
    label = lax.broadcasted_iota(jnp.int32, (F, 1), 0).astype(jnp.float32)
    every = (slot == label).astype(jnp.float32).astype(jnp.bfloat16)
    ones = jnp.ones((16, slot.shape[1]), jnp.bfloat16)
    count = lax.dot_general(ones, every, nt, preferred_element_type=jnp.float32)[0:8]
    sub = lax.broadcasted_iota(jnp.int32, (8, F), 0)
    for y in range(NY):
        mine = relative == float(6 * y)
        a = jnp.where(mine, left_hi, 0.0).astype(jnp.bfloat16)
        b = jnp.where(mine, left_lo, 0.0).astype(jnp.bfloat16)
        wide = lax.dot_general(a, both, nn, preferred_element_type=jnp.float32)
        gram = wide[:, :F] + (
            wide[:, F:] + lax.dot_general(b, hi, nn, preferred_element_type=jnp.float32)
        )
        tile = jnp.where(sub < 6, total[8 * y : 8 * y + 8], count)
        for x in range(NX):
            to = NEAR.index(x * NY + y)
            for i in range(OWN):
                at = (x * OWN + i) * 8
                out_ref[to, i * 8 : i * 8 + 8, :] = gram[at : at + 8]
            out_ref[to, 48:56, :] = tile


def relay_kernel(in_ref, out_ref):
    y, z, c, x = (lax.axis_index(axis) for axis in ALL)
    total = jnp.sum(in_ref[...], axis=0)
    sums, counts = total[48:56], total[54:55]
    q = lax.broadcasted_iota(jnp.int32, (8, 1), 0)
    lane = lax.broadcasted_iota(jnp.int32, (8, F), 1)
    line = 96 * q + 48 * (z & 1) + 24 * c + 6 * x
    head, tail = line >> 7, (line + 5) >> 7

    def pick(which):
        out = jnp.zeros((8, F), jnp.float32)
        for j in range(6):
            out = jnp.where(which == j, sums[j : j + 1], out)
        return out

    def number(which):
        return jnp.sum(jnp.where(lane == which + 6 * y, counts, 0.0), axis=1, keepdims=True)

    def put(i, part):
        out_ref[0 : 8 - Z0, i, :] = part[Z0:]
        out_ref[8 - Z0 :, i, :] = part[:Z0]

    for i in range(OWN):
        part = total[8 * i : 8 * i + 8]
        if i == 1:
            part = jnp.where(lane == (line & 127), number(head), part)
        if i == 5:
            part = jnp.where(lane == ((line + 4) & 127), number(tail), part)
        put(i, part)
    put(6, pick(head))
    put(7, pick(tail))


def final_kernel(in_ref, out_ref):
    z, c, x = lax.axis_index(Z), lax.axis_index(C), lax.axis_index(X)
    total = jnp.sum(in_ref[...], axis=0)
    start = (48 * z + 24 * c + 6 * x) & 127
    lane = lax.broadcasted_iota(jnp.int32, (1, F), 1)

    def entry(row, column):
        return jnp.sum(jnp.where(lane == column, total[row : row + 1], 0.0), axis=1, keepdims=True)

    fifth = (start + 4) & 127
    count_head, count_tail = entry(1, start), entry(5, fifth)
    fix_head, fix_tail = entry(0, start + 1), entry(4, fifth + 1)
    sub = lax.broadcasted_iota(jnp.int32, (8, 1), 0)
    wide = lax.broadcasted_iota(jnp.int32, (8, F), 1)
    gram = jnp.where((sub == 1) & (wide == start), fix_head, total)
    gram = jnp.where((sub == 5) & (wide == fifth), fix_tail, gram)
    in_head = start + sub < F
    slot_total = jnp.where(in_head, total[6:7], total[7:8])
    count = jnp.where(in_head, count_head, count_tail)
    own = jnp.sum(jnp.where(wide == ((start + sub) & 127), slot_total, 0.0), axis=1, keepdims=True)
    result = (gram - own * slot_total / count) / (count - 1.0)
    out_ref[...] = result[0:OWN]


def local(features, key_ids, owner):
    packed = pl.pallas_call(
        pack_kernel,
        out_shape=jax.ShapeDtypeStruct((PACK, F), jnp.float32),
        in_specs=[HBM, HBM, HBM],
        out_specs=VMEM,
        scratch_shapes=[
            pltpu.SMEM((KEYS,), jnp.int32),
            pltpu.VMEM((2, F), jnp.int32),
            pltpu.SemaphoreType.DMA((3,)),
        ],
        compiler_params=PARAMS,
        name="pack",
    )(*(pltpu.with_memory_space_constraint(v, pltpu.HBM) for v in (owner, features, key_ids.reshape(2, F))))
    pair = lax.all_gather(packed, (Z, C), axis_index_groups=PAIRS, tiled=True)
    partial = pl.pallas_call(
        gram_kernel,
        out_shape=jax.ShapeDtypeStruct((NY * NX, MSG, F), jnp.float32),
        in_specs=[VMEM],
        out_specs=VMEM,
        compiler_params=PARAMS,
        name="gram",
    )(pair)
    near = lax.all_to_all(partial, (X, Y), 0, 0, axis_index_groups=[NEAR], tiled=True)
    relayed = pl.pallas_call(
        relay_kernel,
        out_shape=jax.ShapeDtypeStruct((8, 8, F), jnp.float32),
        in_specs=[VMEM],
        out_specs=VMEM,
        compiler_params=PARAMS,
        name="relay",
    )(near)
    far = lax.all_to_all(relayed, Z, 0, 0, axis_index_groups=FAR, tiled=True)
    return pl.pallas_call(
        final_kernel,
        out_shape=jax.ShapeDtypeStruct((OWN, F), jnp.float32),
        in_specs=[VMEM],
        out_specs=VMEM,
        compiler_params=PARAMS,
        name="finish",
    )(far)


def solution(mesh):
    torus = Mesh(mesh.devices.reshape(NY, NZ, 2, NX), ALL)
    in_specs = (P(ALL, None), P(ALL), P())
    return jax.shard_map(local, mesh=torus, in_specs=in_specs, out_specs=P(ALL, None), check_vma=False)
```

```python
import jax
import jax.numpy as jnp
from jax import lax
from jax.experimental import pallas as pl
from jax.experimental.pallas import tpu as pltpu
from jax.sharding import Mesh
from jax.sharding import PartitionSpec as P

Y, Z, C, X = "y", "z", "c", "x"
ALL = (Y, Z, C, X)
F = 128
KEYS = 24
NY, NZ, NX = 4, 16, 4
OWN = 6
PACK = 264
MSG = 56
VMEM = pl.BlockSpec(memory_space=pltpu.VMEM)
HBM = pl.BlockSpec(memory_space=pltpu.HBM)
Y0, Z0, X0 = 2, 5, 2
NEAR = [(i + X0) % NX * NY + (j + Y0) % NY for i in range(NX) for j in range(NY)]
FAR = [[(2 * (k + Z0) + odd) % NZ for k in range(8)] for odd in range(2)]
PAIRS = [[4 * k + j for j in range(4)] for k in range(8)]
PARAMS = pltpu.CompilerParams(vmem_limit_bytes=16 * 1024 * 1024)


def pack_kernel(owner_ref, features_ref, keys_ref, out_ref, owner_buf, keys_buf, sems):
    rows = features_ref.shape[0]
    copies = [
        pltpu.make_async_copy(owner_ref, owner_buf, sems.at[0]),
        pltpu.make_async_copy(keys_ref, keys_buf, sems.at[1]),
        pltpu.make_async_copy(features_ref, out_ref.at[0:rows, :], sems.at[2]),
    ]
    for copy in copies:
        copy.start()
    copies[0].wait()
    copies[1].wait()
    keys = keys_buf[...]
    slot = jnp.zeros(keys.shape, jnp.float32)
    for key in range(KEYS):
        slot = jnp.where(keys == key, owner_buf[key].astype(jnp.float32), slot)
    out_ref[rows:, :] = jnp.concatenate([slot, jnp.zeros((6, F), jnp.float32)], axis=0)
    copies[2].wait()


def gram_kernel(rows_ref, out_ref):
    c, z = lax.axis_index(C), lax.axis_index(Z)
    rows = PACK - 8
    starts = range(0, 4 * PACK, PACK)
    feats = jnp.concatenate([rows_ref[at : at + rows, :] for at in starts], axis=0)
    slots = [rows_ref[at + rows : at + PACK, :] for at in starts]
    slot = jnp.concatenate([s[j : j + 1] for s in slots for j in range(2)], axis=1)
    hi = feats.astype(jnp.bfloat16)
    lo = (feats - hi.astype(jnp.float32)).astype(jnp.bfloat16)
    both = jnp.concatenate([hi, lo], axis=1)

    m = NX * OWN * 8
    index = lax.broadcasted_iota(jnp.int32, (m, 1), 0)
    line = 96 * (index & 7) + 48 * (z & 1) + 24 * c + (index >> 3)
    lane = lax.broadcasted_iota(jnp.int32, (m, F), 1)
    select = (lane == (line & 127)).astype(jnp.float32).astype(jnp.bfloat16)
    nt = (((1,), (1,)), ((), ()))
    nn = (((1,), (0,)), ((), ()))
    left_hi = lax.dot_general(select, hi, nt, preferred_element_type=jnp.float32)
    left_lo = lax.dot_general(select, lo, nt, preferred_element_type=jnp.float32)
    relative = slot - (line >> 7).astype(jnp.float32)

    index = lax.broadcasted_iota(jnp.int32, (32, 1), 0)
    wanted = jnp.where((index & 7) < 6, 6 * (index >> 3) + (index & 7), -1).astype(jnp.float32)
    onehot = (slot == wanted).astype(jnp.float32)
    count = jnp.sum(onehot, axis=1, keepdims=True)

    masks = [relative == float(6 * y) for y in range(NY)]
    a = jnp.concatenate(
        [jnp.where(mine, left_hi, 0.0).astype(jnp.bfloat16) for mine in masks]
        + [onehot.astype(jnp.bfloat16)],
        axis=0,
    )
    b = jnp.concatenate(
        [jnp.where(mine, left_lo, 0.0).astype(jnp.bfloat16) for mine in masks], axis=0
    )
    wide = lax.dot_general(a, both, nn, preferred_element_type=jnp.float32)
    narrow = lax.dot_general(b, hi, nn, preferred_element_type=jnp.float32)
    gram = wide[: NY * m, :F] + (wide[: NY * m, F:] + narrow)
    total = wide[NY * m :, :F] + wide[NY * m :, F:]
    sub = lax.broadcasted_iota(jnp.int32, (8, F), 0)
    lane = lax.broadcasted_iota(jnp.int32, (8, F), 1)
    for y in range(NY):
        own = jnp.sum(
            jnp.where(lane == sub, count[8 * y : 8 * y + 8], 0.0), axis=0, keepdims=True
        )
        tile = jnp.where(sub < 6, total[8 * y : 8 * y + 8], own)
        for x in range(NX):
            to = NEAR.index(x * NY + y)
            for i in range(OWN):
                at = y * m + (x * OWN + i) * 8
                out_ref[to, i * 8 : i * 8 + 8, :] = gram[at : at + 8]
            out_ref[to, 48:56, :] = tile


def relay_kernel(in_ref, out_ref):
    z, c, x = lax.axis_index(Z), lax.axis_index(C), lax.axis_index(X)
    total = jnp.sum(in_ref[...], axis=0)
    sums, counts = total[48:56], total[54:55]
    q = lax.broadcasted_iota(jnp.int32, (8, 1), 0)
    lane = lax.broadcasted_iota(jnp.int32, (8, F), 1)
    line = 96 * q + 48 * (z & 1) + 24 * c + 6 * x
    head, tail = line >> 7, (line + 5) >> 7

    def pick(which):
        out = jnp.zeros((8, F), jnp.float32)
        for j in range(6):
            out = jnp.where(which == j, sums[j : j + 1], out)
        return out

    def number(which):
        return jnp.sum(jnp.where(lane == which, counts, 0.0), axis=1, keepdims=True)

    def put(i, part):
        out_ref[0 : 8 - Z0, i, :] = part[Z0:]
        out_ref[8 - Z0 :, i, :] = part[:Z0]

    for i in range(OWN):
        part = total[8 * i : 8 * i + 8]
        if i == 1:
            part = jnp.where(lane == (line & 127), number(head), part)
        if i == 5:
            part = jnp.where(lane == ((line + 4) & 127), number(tail), part)
        put(i, part)
    put(6, pick(head))
    put(7, pick(tail))


def final_kernel(in_ref, out_ref):
    z, c, x = lax.axis_index(Z), lax.axis_index(C), lax.axis_index(X)
    total = jnp.sum(in_ref[...], axis=0)
    start = (48 * z + 24 * c + 6 * x) & 127
    lane = lax.broadcasted_iota(jnp.int32, (1, F), 1)

    def entry(row, column):
        return jnp.sum(jnp.where(lane == column, total[row : row + 1], 0.0), axis=1, keepdims=True)

    fifth = (start + 4) & 127
    count_head, count_tail = entry(1, start), entry(5, fifth)
    fix_head, fix_tail = entry(0, start + 1), entry(4, fifth + 1)
    sub = lax.broadcasted_iota(jnp.int32, (8, 1), 0)
    wide = lax.broadcasted_iota(jnp.int32, (8, F), 1)
    gram = jnp.where((sub == 1) & (wide == start), fix_head, total)
    gram = jnp.where((sub == 5) & (wide == fifth), fix_tail, gram)
    in_head = start + sub < F
    slot_total = jnp.where(in_head, total[6:7], total[7:8])
    count = jnp.where(in_head, count_head, count_tail)
    own = jnp.sum(jnp.where(wide == ((start + sub) & 127), slot_total, 0.0), axis=1, keepdims=True)
    result = (gram - own * slot_total / count) / (count - 1.0)
    out_ref[...] = result[0:OWN]


def local(features, key_ids, owner):
    packed = pl.pallas_call(
        pack_kernel,
        out_shape=jax.ShapeDtypeStruct((PACK, F), jnp.float32),
        in_specs=[HBM, HBM, HBM],
        out_specs=VMEM,
        scratch_shapes=[
            pltpu.SMEM((KEYS,), jnp.int32),
            pltpu.VMEM((2, F), jnp.int32),
            pltpu.SemaphoreType.DMA((3,)),
        ],
        compiler_params=PARAMS,
        name="pack",
    )(*(pltpu.with_memory_space_constraint(v, pltpu.HBM) for v in (owner, features, key_ids.reshape(2, F))))
    pair = lax.all_gather(packed, (Z, C), axis_index_groups=PAIRS, tiled=True)
    partial = pl.pallas_call(
        gram_kernel,
        out_shape=jax.ShapeDtypeStruct((NY * NX, MSG, F), jnp.float32),
        in_specs=[VMEM],
        out_specs=VMEM,
        compiler_params=PARAMS,
        name="gram",
    )(pair)
    near = lax.all_to_all(partial, (X, Y), 0, 0, axis_index_groups=[NEAR], tiled=True)
    relayed = pl.pallas_call(
        relay_kernel,
        out_shape=jax.ShapeDtypeStruct((8, 8, F), jnp.float32),
        in_specs=[VMEM],
        out_specs=VMEM,
        compiler_params=PARAMS,
        name="relay",
    )(near)
    far = lax.all_to_all(relayed, Z, 0, 0, axis_index_groups=FAR, tiled=True)
    return pl.pallas_call(
        final_kernel,
        out_shape=jax.ShapeDtypeStruct((OWN, F), jnp.float32),
        in_specs=[VMEM],
        out_specs=VMEM,
        compiler_params=PARAMS,
        name="finish",
    )(far)


def solution(mesh):
    torus = Mesh(mesh.devices.reshape(NY, NZ, 2, NX), ALL)
    in_specs = (P(ALL, None), P(ALL), P())
    return jax.shard_map(local, mesh=torus, in_specs=in_specs, out_specs=P(ALL, None), check_vma=False)
```

```python
import jax
import jax.numpy as jnp
from jax import lax
from jax.experimental import pallas as pl
from jax.experimental.pallas import tpu as pltpu
from jax.sharding import Mesh
from jax.sharding import PartitionSpec as P

Y, Z, C, X = "y", "z", "c", "x"
ALL = (Y, Z, C, X)
F = 128
KEYS = 24
NY, NZ, NX = 4, 16, 4
OWN = 6
PACK = 264
MSG = 56
VMEM = pl.BlockSpec(memory_space=pltpu.VMEM)
HBM = pl.BlockSpec(memory_space=pltpu.HBM)
Y0, Z0, X0 = 2, 5, 2
NEAR = [(i + X0) % NX * NY + (j + Y0) % NY for i in range(NX) for j in range(NY)]
FAR = [[(2 * (k + Z0) + odd) % NZ for k in range(8)] for odd in range(2)]
PAIRS = [[4 * k + j for j in range(4)] for k in range(8)]
PARAMS = pltpu.CompilerParams(vmem_limit_bytes=16 * 1024 * 1024)


def pack_kernel(owner_ref, features_ref, keys_ref, out_ref, owner_buf, keys_buf, sems):
    rows = features_ref.shape[0]
    copies = [
        pltpu.make_async_copy(owner_ref, owner_buf, sems.at[0]),
        pltpu.make_async_copy(keys_ref, keys_buf, sems.at[1]),
        pltpu.make_async_copy(features_ref, out_ref.at[0:rows, :], sems.at[2]),
    ]
    for copy in copies:
        copy.start()
    copies[0].wait()
    copies[1].wait()
    keys = keys_buf[...]
    slot = jnp.zeros(keys.shape, jnp.float32)
    for key in range(KEYS):
        slot = jnp.where(keys == key, owner_buf[key].astype(jnp.float32), slot)
    out_ref[rows:, :] = jnp.concatenate([slot, jnp.zeros((6, F), jnp.float32)], axis=0)
    copies[2].wait()


def gram_kernel(rows_ref, out_ref):
    c, z = lax.axis_index(C), lax.axis_index(Z)
    rows = PACK - 8
    starts = range(0, 4 * PACK, PACK)
    feats = jnp.concatenate([rows_ref[at : at + rows, :] for at in starts], axis=0)
    slots = [rows_ref[at + rows : at + PACK, :] for at in starts]
    slot = jnp.concatenate([s[j : j + 1] for s in slots for j in range(2)], axis=1)
    hi = feats.astype(jnp.bfloat16)
    lo = (feats - hi.astype(jnp.float32)).astype(jnp.bfloat16)
    both = jnp.concatenate([hi, lo], axis=1)

    m = NX * OWN * 8
    index = lax.broadcasted_iota(jnp.int32, (m, 1), 0)
    line = 96 * (index & 7) + 48 * (z & 1) + 24 * c + (index >> 3)
    lane = lax.broadcasted_iota(jnp.int32, (m, F), 1)
    select = (lane == (line & 127)).astype(jnp.float32).astype(jnp.bfloat16)
    nt = (((1,), (1,)), ((), ()))
    nn = (((1,), (0,)), ((), ()))
    left_hi = lax.dot_general(select, hi, nt, preferred_element_type=jnp.float32)
    left_lo = lax.dot_general(select, lo, nt, preferred_element_type=jnp.float32)
    relative = slot - (line >> 7).astype(jnp.float32)

    index = lax.broadcasted_iota(jnp.int32, (32, 1), 0)
    wanted = jnp.where((index & 7) < 6, 6 * (index >> 3) + (index & 7), -1).astype(jnp.float32)
    onehot = (slot == wanted).astype(jnp.float32)
    count = jnp.sum(onehot, axis=1, keepdims=True)

    masks = [relative == float(6 * y) for y in range(NY)]
    a = jnp.concatenate(
        [jnp.where(mine, left_hi, 0.0).astype(jnp.bfloat16) for mine in masks]
        + [onehot.astype(jnp.bfloat16)],
        axis=0,
    )
    b = jnp.concatenate(
        [jnp.where(mine, left_lo, 0.0).astype(jnp.bfloat16) for mine in masks], axis=0
    )
    wide = lax.dot_general(a, both, nn, preferred_element_type=jnp.float32)
    fine = lax.dot_general(b, both, nn, preferred_element_type=jnp.float32)
    gram = wide[: NY * m, :F] + (wide[: NY * m, F:] + (fine[:, :F] + fine[:, F:]))
    total = wide[NY * m :, :F] + wide[NY * m :, F:]
    sub = lax.broadcasted_iota(jnp.int32, (8, F), 0)
    lane = lax.broadcasted_iota(jnp.int32, (8, F), 1)
    for y in range(NY):
        own = jnp.sum(
            jnp.where(lane == sub, count[8 * y : 8 * y + 8], 0.0), axis=0, keepdims=True
        )
        tile = jnp.where(sub < 6, total[8 * y : 8 * y + 8], own)
        for x in range(NX):
            to = NEAR.index(x * NY + y)
            for i in range(OWN):
                at = y * m + (x * OWN + i) * 8
                out_ref[to, i * 8 : i * 8 + 8, :] = gram[at : at + 8]
            out_ref[to, 48:56, :] = tile


def relay_kernel(in_ref, out_ref):
    z, c, x = lax.axis_index(Z), lax.axis_index(C), lax.axis_index(X)
    total = jnp.sum(in_ref[...], axis=0)
    sums, counts = total[48:56], total[54:55]
    q = lax.broadcasted_iota(jnp.int32, (8, 1), 0)
    lane = lax.broadcasted_iota(jnp.int32, (8, F), 1)
    line = 96 * q + 48 * (z & 1) + 24 * c + 6 * x
    head, tail = line >> 7, (line + 5) >> 7

    def pick(which):
        out = jnp.zeros((8, F), jnp.float32)
        for j in range(6):
            out = jnp.where(which == j, sums[j : j + 1], out)
        return out

    def number(which):
        return jnp.sum(jnp.where(lane == which, counts, 0.0), axis=1, keepdims=True)

    def put(i, part):
        out_ref[0 : 8 - Z0, i, :] = part[Z0:]
        out_ref[8 - Z0 :, i, :] = part[:Z0]

    for i in range(OWN):
        part = total[8 * i : 8 * i + 8]
        if i == 1:
            part = jnp.where(lane == (line & 127), number(head), part)
        if i == 5:
            part = jnp.where(lane == ((line + 4) & 127), number(tail), part)
        put(i, part)
    put(6, pick(head))
    put(7, pick(tail))


def final_kernel(in_ref, out_ref):
    z, c, x = lax.axis_index(Z), lax.axis_index(C), lax.axis_index(X)
    total = jnp.sum(in_ref[...], axis=0)
    start = (48 * z + 24 * c + 6 * x) & 127
    lane = lax.broadcasted_iota(jnp.int32, (1, F), 1)

    def entry(row, column):
        return jnp.sum(jnp.where(lane == column, total[row : row + 1], 0.0), axis=1, keepdims=True)

    fifth = (start + 4) & 127
    count_head, count_tail = entry(1, start), entry(5, fifth)
    fix_head, fix_tail = entry(0, start + 1), entry(4, fifth + 1)
    sub = lax.broadcasted_iota(jnp.int32, (8, 1), 0)
    wide = lax.broadcasted_iota(jnp.int32, (8, F), 1)
    gram = jnp.where((sub == 1) & (wide == start), fix_head, total)
    gram = jnp.where((sub == 5) & (wide == fifth), fix_tail, gram)
    in_head = start + sub < F
    slot_total = jnp.where(in_head, total[6:7], total[7:8])
    count = jnp.where(in_head, count_head, count_tail)
    own = jnp.sum(jnp.where(wide == ((start + sub) & 127), slot_total, 0.0), axis=1, keepdims=True)
    result = (gram - own * slot_total / count) / (count - 1.0)
    out_ref[...] = result[0:OWN]


def local(features, key_ids, owner):
    packed = pl.pallas_call(
        pack_kernel,
        out_shape=jax.ShapeDtypeStruct((PACK, F), jnp.float32),
        in_specs=[HBM, HBM, HBM],
        out_specs=VMEM,
        scratch_shapes=[
            pltpu.SMEM((KEYS,), jnp.int32),
            pltpu.VMEM((2, F), jnp.int32),
            pltpu.SemaphoreType.DMA((3,)),
        ],
        compiler_params=PARAMS,
        name="pack",
    )(*(pltpu.with_memory_space_constraint(v, pltpu.HBM) for v in (owner, features, key_ids.reshape(2, F))))
    pair = lax.all_gather(packed, (Z, C), axis_index_groups=PAIRS, tiled=True)
    partial = pl.pallas_call(
        gram_kernel,
        out_shape=jax.ShapeDtypeStruct((NY * NX, MSG, F), jnp.float32),
        in_specs=[VMEM],
        out_specs=VMEM,
        compiler_params=PARAMS,
        name="gram",
    )(pair)
    near = lax.all_to_all(partial, (X, Y), 0, 0, axis_index_groups=[NEAR], tiled=True)
    relayed = pl.pallas_call(
        relay_kernel,
        out_shape=jax.ShapeDtypeStruct((8, 8, F), jnp.float32),
        in_specs=[VMEM],
        out_specs=VMEM,
        compiler_params=PARAMS,
        name="relay",
    )(near)
    far = lax.all_to_all(relayed, Z, 0, 0, axis_index_groups=FAR, tiled=True)
    return pl.pallas_call(
        final_kernel,
        out_shape=jax.ShapeDtypeStruct((OWN, F), jnp.float32),
        in_specs=[VMEM],
        out_specs=VMEM,
        compiler_params=PARAMS,
        name="finish",
    )(far)


def solution(mesh):
    torus = Mesh(mesh.devices.reshape(NY, NZ, 2, NX), ALL)
    in_specs = (P(ALL, None), P(ALL), P())
    return jax.shard_map(local, mesh=torus, in_specs=in_specs, out_specs=P(ALL, None), check_vma=False)
```

```python
import jax
import jax.numpy as jnp
from jax import lax
from jax.experimental import pallas as pl
from jax.experimental.pallas import tpu as pltpu
from jax.sharding import Mesh
from jax.sharding import PartitionSpec as P

Y, Z, C, X = "y", "z", "c", "x"
ALL = (Y, Z, C, X)
F = 128
KEYS = 24
NY, NZ, NX = 4, 16, 4
OWN = 6
PACK = 264
PARTS = 4
MSG = 56
VMEM = pl.BlockSpec(memory_space=pltpu.VMEM)
HBM = pl.BlockSpec(memory_space=pltpu.HBM)
Y0, Z0, X0 = 2, 5, 2
NEAR = [(i + X0) % NX * NY + (j + Y0) % NY for i in range(NX) for j in range(NY)]
FAR = [[(2 * (k + Z0) + odd) % NZ for k in range(8)] for odd in range(2)]
PAIRS = [[4 * k + j for j in range(4)] for k in range(8)]
PARAMS = pltpu.CompilerParams(vmem_limit_bytes=16 * 1024 * 1024)


def pack_kernel(owner_ref, features_ref, keys_ref, out_ref, owner_buf, keys_buf, sems):
    rows = features_ref.shape[0]
    copies = [
        pltpu.make_async_copy(owner_ref, owner_buf, sems.at[0]),
        pltpu.make_async_copy(keys_ref, keys_buf, sems.at[1]),
    ]
    step = rows // PARTS
    for part in range(PARTS):
        lines = pl.ds(part * step, step)
        copies.append(
            pltpu.make_async_copy(features_ref.at[lines, :], out_ref.at[lines, :], sems.at[2 + part])
        )
    for copy in copies:
        copy.start()
    copies[0].wait()
    copies[1].wait()
    keys = keys_buf[...]
    slot = jnp.zeros(keys.shape, jnp.float32)
    for key in range(KEYS):
        slot = jnp.where(keys == key, owner_buf[key].astype(jnp.float32), slot)
    out_ref[rows:, :] = jnp.concatenate([slot, jnp.zeros((6, F), jnp.float32)], axis=0)
    for copy in copies[2:]:
        copy.wait()


def gram_kernel(rows_ref, out_ref):
    c, z = lax.axis_index(C), lax.axis_index(Z)
    rows = PACK - 8
    starts = range(0, 4 * PACK, PACK)
    feats = jnp.concatenate([rows_ref[at : at + rows, :] for at in starts], axis=0)
    slots = [rows_ref[at + rows : at + PACK, :] for at in starts]
    slot = jnp.concatenate([s[j : j + 1] for s in slots for j in range(2)], axis=1)
    hi = feats.astype(jnp.bfloat16)
    lo = (feats - hi.astype(jnp.float32)).astype(jnp.bfloat16)
    both = jnp.concatenate([hi, lo], axis=1)

    m = NX * OWN * 4
    index = lax.broadcasted_iota(jnp.int32, (m, 1), 0)
    line = 96 * (index & 3) + 48 * (z & 1) + 24 * c + (index >> 2)
    lane = lax.broadcasted_iota(jnp.int32, (m, F), 1)
    select = (lane == (line & 127)).astype(jnp.float32).astype(jnp.bfloat16)
    nt = (((1,), (1,)), ((), ()))
    nn = (((1,), (0,)), ((), ()))
    left_hi = lax.dot_general(select, hi, nt, preferred_element_type=jnp.float32)
    left_hi = left_hi.astype(jnp.bfloat16)
    left_lo = lax.dot_general(select, lo, nt, preferred_element_type=jnp.float32)
    left_lo = left_lo.astype(jnp.bfloat16)
    relative = (slot - (line >> 7).astype(jnp.float32)).astype(jnp.bfloat16)

    index = lax.broadcasted_iota(jnp.int32, (32, 1), 0)
    wanted = jnp.where((index & 7) < 6, 6 * (index >> 3) + (index & 7), -1).astype(jnp.float32)
    onehot = (slot == wanted).astype(jnp.float32)
    count = jnp.sum(onehot, axis=1, keepdims=True)

    zero = jnp.zeros((), jnp.bfloat16)
    masks = [relative == jnp.bfloat16(3 * group) for group in range(2 * NY)]
    a = jnp.concatenate(
        [jnp.where(mine, left_hi, zero) for mine in masks]
        + [onehot.astype(jnp.bfloat16)],
        axis=0,
    )
    b = jnp.concatenate(
        [jnp.where(mine, left_lo, zero) for mine in masks], axis=0
    )
    wide = lax.dot_general(a, both, nn, preferred_element_type=jnp.float32)
    fine = lax.dot_general(b, both, nn, preferred_element_type=jnp.float32)
    gram = wide[: 2 * NY * m, :F] + (wide[: 2 * NY * m, F:] + (fine[:, :F] + fine[:, F:]))
    total = wide[2 * NY * m :, :F] + wide[2 * NY * m :, F:]
    sub = lax.broadcasted_iota(jnp.int32, (8, F), 0)
    lane = lax.broadcasted_iota(jnp.int32, (8, F), 1)
    for y in range(NY):
        own = jnp.sum(
            jnp.where(lane == sub, count[8 * y : 8 * y + 8], 0.0), axis=0, keepdims=True
        )
        tile = jnp.where(sub < 6, total[8 * y : 8 * y + 8], own)
        for x in range(NX):
            to = NEAR.index(x * NY + y)
            for half in range(2):
                at = (2 * y + half) * m + x * 24
                out_ref[to, half * 24 : half * 24 + 24, :] = gram[at : at + 24]
            out_ref[to, 48:56, :] = tile


def relay_kernel(in_ref, out_ref):
    z, c, x = lax.axis_index(Z), lax.axis_index(C), lax.axis_index(X)
    total = jnp.sum(in_ref[...], axis=0)
    sums, counts = total[48:56], total[54:55]
    q = lax.broadcasted_iota(jnp.int32, (8, 1), 0)
    lane = lax.broadcasted_iota(jnp.int32, (8, F), 1)
    line = 96 * q + 48 * (z & 1) + 24 * c + 6 * x
    head, tail = line >> 7, (line + 5) >> 7

    def pick(which):
        out = jnp.zeros((8, F), jnp.float32)
        for j in range(6):
            out = jnp.where(which == j, sums[j : j + 1], out)
        return out

    def number(which):
        return jnp.sum(jnp.where(lane == which, counts, 0.0), axis=1, keepdims=True)

    def put(i, part):
        out_ref[0 : 8 - Z0, i, :] = part[Z0:]
        out_ref[8 - Z0 :, i, :] = part[:Z0]

    for i in range(OWN):
        part = jnp.concatenate([total[4 * i : 4 * i + 4], total[24 + 4 * i : 28 + 4 * i]], axis=0)
        if i == 1:
            part = jnp.where(lane == (line & 127), number(head), part)
        if i == 5:
            part = jnp.where(lane == ((line + 4) & 127), number(tail), part)
        put(i, part)
    put(6, pick(head))
    put(7, pick(tail))


def final_kernel(in_ref, out_ref):
    z, c, x = lax.axis_index(Z), lax.axis_index(C), lax.axis_index(X)
    total = jnp.sum(in_ref[...], axis=0)
    start = (48 * z + 24 * c + 6 * x) & 127
    lane = lax.broadcasted_iota(jnp.int32, (1, F), 1)

    def entry(row, column):
        return jnp.sum(jnp.where(lane == column, total[row : row + 1], 0.0), axis=1, keepdims=True)

    fifth = (start + 4) & 127
    count_head, count_tail = entry(1, start), entry(5, fifth)
    fix_head, fix_tail = entry(0, start + 1), entry(4, fifth + 1)
    sub = lax.broadcasted_iota(jnp.int32, (8, 1), 0)
    wide = lax.broadcasted_iota(jnp.int32, (8, F), 1)
    gram = jnp.where((sub == 1) & (wide == start), fix_head, total)
    gram = jnp.where((sub == 5) & (wide == fifth), fix_tail, gram)
    in_head = start + sub < F
    slot_total = jnp.where(in_head, total[6:7], total[7:8])
    count = jnp.where(in_head, count_head, count_tail)
    own = jnp.sum(jnp.where(wide == ((start + sub) & 127), slot_total, 0.0), axis=1, keepdims=True)
    result = (gram - own * slot_total / count) / (count - 1.0)
    out_ref[...] = result[0:OWN]


def local(features, key_ids, owner):
    packed = pl.pallas_call(
        pack_kernel,
        out_shape=jax.ShapeDtypeStruct((PACK, F), jnp.float32),
        in_specs=[HBM, HBM, HBM],
        out_specs=VMEM,
        scratch_shapes=[
            pltpu.SMEM((KEYS,), jnp.int32),
            pltpu.VMEM((2, F), jnp.int32),
            pltpu.SemaphoreType.DMA((2 + PARTS,)),
        ],
        compiler_params=PARAMS,
        name="pack",
    )(*(pltpu.with_memory_space_constraint(v, pltpu.HBM) for v in (owner, features, key_ids.reshape(2, F))))
    pair = lax.all_gather(packed, (Z, C), axis_index_groups=PAIRS, tiled=True)
    partial = pl.pallas_call(
        gram_kernel,
        out_shape=jax.ShapeDtypeStruct((NY * NX, MSG, F), jnp.float32),
        in_specs=[VMEM],
        out_specs=VMEM,
        compiler_params=PARAMS,
        name="gram",
    )(pair)
    near = lax.all_to_all(partial, (X, Y), 0, 0, axis_index_groups=[NEAR], tiled=True)
    relayed = pl.pallas_call(
        relay_kernel,
        out_shape=jax.ShapeDtypeStruct((8, 8, F), jnp.float32),
        in_specs=[VMEM],
        out_specs=VMEM,
        compiler_params=PARAMS,
        name="relay",
    )(near)
    far = lax.all_to_all(relayed, Z, 0, 0, axis_index_groups=FAR, tiled=True)
    return pl.pallas_call(
        final_kernel,
        out_shape=jax.ShapeDtypeStruct((OWN, F), jnp.float32),
        in_specs=[VMEM],
        out_specs=VMEM,
        compiler_params=PARAMS,
        name="finish",
    )(far)


def solution(mesh):
    torus = Mesh(mesh.devices.reshape(NY, NZ, 2, NX), ALL)
    in_specs = (P(ALL, None), P(ALL), P())
    return jax.shard_map(local, mesh=torus, in_specs=in_specs, out_specs=P(ALL, None), check_vma=False)
```

```python
import jax
import jax.numpy as jnp
from jax import lax
from jax.experimental import pallas as pl
from jax.experimental.pallas import tpu as pltpu
from jax.sharding import Mesh
from jax.sharding import PartitionSpec as P

Y, Z, C, X = "y", "z", "c", "x"
ALL = (Y, Z, C, X)
F = 128
KEYS = 24
NY, NZ, NX = 4, 16, 4
OWN = 6
PACK = 264
PARTS = 4
MSG = 56
VMEM = pl.BlockSpec(memory_space=pltpu.VMEM)
HBM = pl.BlockSpec(memory_space=pltpu.HBM)
Y0, Z0, X0 = 2, 4, 2
NEAR = [(i + X0) % NX * NY + (j + Y0) % NY for i in range(NX) for j in range(NY)]
FAR = [[(2 * (k + Z0) + odd) % NZ for k in range(8)] for odd in range(2)]
PAIRS = [[4 * k + j for j in range(4)] for k in range(8)]
PARAMS = pltpu.CompilerParams(vmem_limit_bytes=16 * 1024 * 1024)


def pack_kernel(owner_ref, features_ref, keys_ref, out_ref, owner_buf, keys_buf, sems):
    rows = features_ref.shape[0]
    copies = [
        pltpu.make_async_copy(owner_ref, owner_buf, sems.at[0]),
        pltpu.make_async_copy(keys_ref, keys_buf, sems.at[1]),
    ]
    step = rows // PARTS
    for part in range(PARTS):
        lines = pl.ds(part * step, step)
        copies.append(
            pltpu.make_async_copy(features_ref.at[lines, :], out_ref.at[lines, :], sems.at[2 + part])
        )
    for copy in copies:
        copy.start()
    copies[0].wait()
    copies[1].wait()
    keys = keys_buf[...]
    slot = jnp.zeros(keys.shape, jnp.float32)
    for key in range(KEYS):
        slot = jnp.where(keys == key, owner_buf[key].astype(jnp.float32), slot)
    out_ref[rows:, :] = jnp.concatenate([slot, jnp.zeros((6, F), jnp.float32)], axis=0)
    for copy in copies[2:]:
        copy.wait()


def gram_kernel(rows_ref, out_ref):
    c, z = lax.axis_index(C), lax.axis_index(Z)
    rows = PACK - 8
    starts = range(0, 4 * PACK, PACK)
    feats = jnp.concatenate([rows_ref[at : at + rows, :] for at in starts], axis=0)
    slots = [rows_ref[at + rows : at + PACK, :] for at in starts]
    slot = jnp.concatenate([s[j : j + 1] for s in slots for j in range(2)], axis=1)
    hi = feats.astype(jnp.bfloat16)
    lo = (feats - hi.astype(jnp.float32)).astype(jnp.bfloat16)
    both = jnp.concatenate([hi, lo], axis=1)

    m = NX * OWN * 4
    index = lax.broadcasted_iota(jnp.int32, (m, 1), 0)
    line = 96 * (index & 3) + 48 * (z & 1) + 24 * c + (index >> 2)
    lane = lax.broadcasted_iota(jnp.int32, (m, F), 1)
    select = (lane == (line & 127)).astype(jnp.float32).astype(jnp.bfloat16)
    nt = (((1,), (1,)), ((), ()))
    nn = (((1,), (0,)), ((), ()))
    left_hi = lax.dot_general(select, hi, nt, preferred_element_type=jnp.float32)
    left_hi = left_hi.astype(jnp.bfloat16)
    left_lo = lax.dot_general(select, lo, nt, preferred_element_type=jnp.float32)
    left_lo = left_lo.astype(jnp.bfloat16)
    relative = (slot - (line >> 7).astype(jnp.float32)).astype(jnp.bfloat16)

    index = lax.broadcasted_iota(jnp.int32, (32, 1), 0)
    wanted = jnp.where((index & 7) < 6, 6 * (index >> 3) + (index & 7), -1).astype(jnp.float32)
    onehot = (slot == wanted).astype(jnp.float32)
    count = jnp.sum(onehot, axis=1, keepdims=True)

    zero = jnp.zeros((), jnp.bfloat16)
    masks = [relative == jnp.bfloat16(3 * group) for group in range(2 * NY)]
    a = jnp.concatenate(
        [jnp.where(mine, left_hi, zero) for mine in masks]
        + [onehot.astype(jnp.bfloat16)],
        axis=0,
    )
    b = jnp.concatenate(
        [jnp.where(mine, left_lo, zero) for mine in masks], axis=0
    )
    wide = lax.dot_general(a, both, nn, preferred_element_type=jnp.float32)
    fine = lax.dot_general(b, both, nn, preferred_element_type=jnp.float32)
    gram = wide[: 2 * NY * m, :F] + (wide[: 2 * NY * m, F:] + (fine[:, :F] + fine[:, F:]))
    total = wide[2 * NY * m :, :F] + wide[2 * NY * m :, F:]
    sub = lax.broadcasted_iota(jnp.int32, (8, F), 0)
    lane = lax.broadcasted_iota(jnp.int32, (8, F), 1)
    for y in range(NY):
        own = jnp.sum(
            jnp.where(lane == sub, count[8 * y : 8 * y + 8], 0.0), axis=0, keepdims=True
        )
        tile = jnp.where(sub < 6, total[8 * y : 8 * y + 8], own)
        for x in range(NX):
            to = NEAR.index(x * NY + y)
            for half in range(2):
                at = (2 * y + half) * m + x * 24
                out_ref[to, half * 24 : half * 24 + 24, :] = gram[at : at + 24]
            out_ref[to, 48:56, :] = tile


def relay_kernel(in_ref, out_ref):
    z, c, x = lax.axis_index(Z), lax.axis_index(C), lax.axis_index(X)
    total = jnp.sum(in_ref[...], axis=0)
    sums, counts = total[48:56], total[54:55]
    q = lax.broadcasted_iota(jnp.int32, (8, 1), 0)
    lane = lax.broadcasted_iota(jnp.int32, (8, F), 1)
    line = 96 * q + 48 * (z & 1) + 24 * c + 6 * x
    head, tail = line >> 7, (line + 5) >> 7

    def pick(which):
        out = jnp.zeros((8, F), jnp.float32)
        for j in range(6):
            out = jnp.where(which == j, sums[j : j + 1], out)
        return out

    def number(which):
        return jnp.sum(jnp.where(lane == which, counts, 0.0), axis=1, keepdims=True)

    def put(i, part):
        out_ref[0 : 8 - Z0, i, :] = part[Z0:]
        out_ref[8 - Z0 :, i, :] = part[:Z0]

    for i in range(OWN):
        part = jnp.concatenate([total[4 * i : 4 * i + 4], total[24 + 4 * i : 28 + 4 * i]], axis=0)
        if i == 1:
            part = jnp.where(lane == (line & 127), number(head), part)
        if i == 5:
            part = jnp.where(lane == ((line + 4) & 127), number(tail), part)
        put(i, part)
    put(6, pick(head))
    put(7, pick(tail))


def final_kernel(in_ref, out_ref):
    z, c, x = lax.axis_index(Z), lax.axis_index(C), lax.axis_index(X)
    total = jnp.sum(in_ref[...], axis=0)
    start = (48 * z + 24 * c + 6 * x) & 127
    lane = lax.broadcasted_iota(jnp.int32, (1, F), 1)

    def entry(row, column):
        return jnp.sum(jnp.where(lane == column, total[row : row + 1], 0.0), axis=1, keepdims=True)

    fifth = (start + 4) & 127
    count_head, count_tail = entry(1, start), entry(5, fifth)
    fix_head, fix_tail = entry(0, start + 1), entry(4, fifth + 1)
    sub = lax.broadcasted_iota(jnp.int32, (8, 1), 0)
    wide = lax.broadcasted_iota(jnp.int32, (8, F), 1)
    gram = jnp.where((sub == 1) & (wide == start), fix_head, total)
    gram = jnp.where((sub == 5) & (wide == fifth), fix_tail, gram)
    in_head = start + sub < F
    slot_total = jnp.where(in_head, total[6:7], total[7:8])
    count = jnp.where(in_head, count_head, count_tail)
    own = jnp.sum(jnp.where(wide == ((start + sub) & 127), slot_total, 0.0), axis=1, keepdims=True)
    result = (gram - own * slot_total / count) / (count - 1.0)
    out_ref[...] = result[0:OWN]


def local(features, key_ids, owner):
    packed = pl.pallas_call(
        pack_kernel,
        out_shape=jax.ShapeDtypeStruct((PACK, F), jnp.float32),
        in_specs=[HBM, HBM, HBM],
        out_specs=VMEM,
        scratch_shapes=[
            pltpu.SMEM((KEYS,), jnp.int32),
            pltpu.VMEM((2, F), jnp.int32),
            pltpu.SemaphoreType.DMA((2 + PARTS,)),
        ],
        compiler_params=PARAMS,
        name="pack",
    )(*(pltpu.with_memory_space_constraint(v, pltpu.HBM) for v in (owner, features, key_ids.reshape(2, F))))
    pair = lax.all_gather(packed, (Z, C), axis_index_groups=PAIRS, tiled=True)
    partial = pl.pallas_call(
        gram_kernel,
        out_shape=jax.ShapeDtypeStruct((NY * NX, MSG, F), jnp.float32),
        in_specs=[VMEM],
        out_specs=VMEM,
        compiler_params=PARAMS,
        name="gram",
    )(pair)
    near = lax.all_to_all(partial, (X, Y), 0, 0, axis_index_groups=[NEAR], tiled=True)
    relayed = pl.pallas_call(
        relay_kernel,
        out_shape=jax.ShapeDtypeStruct((8, 8, F), jnp.float32),
        in_specs=[VMEM],
        out_specs=VMEM,
        compiler_params=PARAMS,
        name="relay",
    )(near)
    far = lax.all_to_all(relayed, Z, 0, 0, axis_index_groups=FAR, tiled=True)
    return pl.pallas_call(
        final_kernel,
        out_shape=jax.ShapeDtypeStruct((OWN, F), jnp.float32),
        in_specs=[VMEM],
        out_specs=VMEM,
        compiler_params=PARAMS,
        name="finish",
    )(far)


def solution(mesh):
    torus = Mesh(mesh.devices.reshape(NY, NZ, 2, NX), ALL)
    in_specs = (P(ALL, None), P(ALL), P())
    return jax.shard_map(local, mesh=torus, in_specs=in_specs, out_specs=P(ALL, None), check_vma=False)
```

```python
import jax
import jax.numpy as jnp
from jax import lax
from jax.experimental import pallas as pl
from jax.experimental.pallas import tpu as pltpu
from jax.sharding import Mesh
from jax.sharding import PartitionSpec as P

Y, Z, C, X = "y", "z", "c", "x"
ALL = (Y, Z, C, X)
F = 128
KEYS = 24
NY, NZ, NX = 4, 16, 4
OWN = 6
PACK = 264
PARTS = 4
MSG = 56
VMEM = pl.BlockSpec(memory_space=pltpu.VMEM)
HBM = pl.BlockSpec(memory_space=pltpu.HBM)
Y0, Z0, X0 = 2, 5, 2
NEAR = [(i + X0) % NX * NY + (j + Y0) % NY for i in range(NX) for j in range(NY)]
FAR = [[(2 * (k + Z0) + odd) % NZ for k in range(8)] for odd in range(2)]
PAIRS = [[4 * k + j for j in range(4)] for k in range(8)]
PARAMS = pltpu.CompilerParams(vmem_limit_bytes=16 * 1024 * 1024)


def pack_kernel(owner_ref, features_ref, keys_ref, out_ref, owner_buf, keys_buf, sems):
    rows = features_ref.shape[0]
    copies = [
        pltpu.make_async_copy(owner_ref, owner_buf, sems.at[0]),
        pltpu.make_async_copy(keys_ref, keys_buf, sems.at[1]),
    ]
    step = rows // PARTS
    for part in range(PARTS):
        lines = pl.ds(part * step, step)
        copies.append(
            pltpu.make_async_copy(features_ref.at[lines, :], out_ref.at[lines, :], sems.at[2 + part])
        )
    for copy in copies:
        copy.start()
    copies[0].wait()
    copies[1].wait()
    keys = keys_buf[...]
    slot = jnp.zeros(keys.shape, jnp.float32)
    for key in range(KEYS):
        slot = jnp.where(keys == key, owner_buf[key].astype(jnp.float32), slot)
    out_ref[rows:, :] = jnp.concatenate([slot, jnp.zeros((6, F), jnp.float32)], axis=0)
    for copy in copies[2:]:
        copy.wait()


def gram_kernel(rows_ref, out_ref):
    c, z = lax.axis_index(C), lax.axis_index(Z)
    rows = PACK - 8
    starts = range(0, 4 * PACK, PACK)
    feats = jnp.concatenate([rows_ref[at : at + rows, :] for at in starts], axis=0)
    slots = [rows_ref[at + rows : at + PACK, :] for at in starts]
    slot = jnp.concatenate([s[j : j + 1] for s in slots for j in range(2)], axis=1)
    hi = feats.astype(jnp.bfloat16)
    lo = (feats - hi.astype(jnp.float32)).astype(jnp.bfloat16)
    both = jnp.concatenate([hi, lo], axis=1)

    m = NX * OWN * 8
    index = lax.broadcasted_iota(jnp.int32, (m, 1), 0)
    line = 96 * (index & 7) + 48 * (z & 1) + 24 * c + (index >> 3)
    lane = lax.broadcasted_iota(jnp.int32, (m, F), 1)
    select = (lane == (line & 127)).astype(jnp.float32).astype(jnp.bfloat16)
    nt = (((1,), (1,)), ((), ()))
    nn = (((1,), (0,)), ((), ()))
    left_hi = lax.dot_general(select, hi, nt, preferred_element_type=jnp.float32)
    left_lo = lax.dot_general(select, lo, nt, preferred_element_type=jnp.float32)
    relative = slot - (line >> 7).astype(jnp.float32)

    index = lax.broadcasted_iota(jnp.int32, (32, 1), 0)
    wanted = jnp.where((index & 7) < 6, 6 * (index >> 3) + (index & 7), -1).astype(jnp.float32)
    onehot = (slot == wanted).astype(jnp.float32)
    count = jnp.sum(onehot, axis=1, keepdims=True)

    masks = [relative == float(6 * y) for y in range(NY)]
    a = jnp.concatenate(
        [jnp.where(mine, left_hi, 0.0).astype(jnp.bfloat16) for mine in masks]
        + [onehot.astype(jnp.bfloat16)],
        axis=0,
    )
    b = jnp.concatenate(
        [jnp.where(mine, left_lo, 0.0).astype(jnp.bfloat16) for mine in masks], axis=0
    )
    wide = lax.dot_general(a, both, nn, preferred_element_type=jnp.float32)
    fine = lax.dot_general(b, both, nn, preferred_element_type=jnp.float32)
    gram = wide[: NY * m, :F] + (wide[: NY * m, F:] + (fine[:, :F] + fine[:, F:]))
    total = wide[NY * m :, :F] + wide[NY * m :, F:]
    sub = lax.broadcasted_iota(jnp.int32, (8, F), 0)
    lane = lax.broadcasted_iota(jnp.int32, (8, F), 1)
    for y in range(NY):
        own = jnp.sum(
            jnp.where(lane == sub, count[8 * y : 8 * y + 8], 0.0), axis=0, keepdims=True
        )
        tile = jnp.where(sub < 6, total[8 * y : 8 * y + 8], own)
        for x in range(NX):
            to = NEAR.index(x * NY + y)
            for i in range(OWN):
                at = y * m + (x * OWN + i) * 8
                out_ref[to, i * 8 : i * 8 + 8, :] = gram[at : at + 8]
            out_ref[to, 48:56, :] = tile


def relay_kernel(in_ref, out_ref):
    z, c, x = lax.axis_index(Z), lax.axis_index(C), lax.axis_index(X)
    total = jnp.sum(in_ref[...], axis=0)
    sums, counts = total[48:56], total[54:55]
    q = lax.broadcasted_iota(jnp.int32, (8, 1), 0)
    lane = lax.broadcasted_iota(jnp.int32, (8, F), 1)
    line = 96 * q + 48 * (z & 1) + 24 * c + 6 * x
    head, tail = line >> 7, (line + 5) >> 7

    def pick(which):
        out = jnp.zeros((8, F), jnp.float32)
        for j in range(6):
            out = jnp.where(which == j, sums[j : j + 1], out)
        return out

    def number(which):
        return jnp.sum(jnp.where(lane == which, counts, 0.0), axis=1, keepdims=True)

    def put(i, part):
        out_ref[0 : 8 - Z0, i, :] = part[Z0:]
        out_ref[8 - Z0 :, i, :] = part[:Z0]

    for i in range(OWN):
        part = total[8 * i : 8 * i + 8]
        if i == 1:
            part = jnp.where(lane == (line & 127), number(head), part)
        if i == 5:
            part = jnp.where(lane == ((line + 4) & 127), number(tail), part)
        put(i, part)
    put(6, pick(head))
    put(7, pick(tail))


def final_kernel(in_ref, out_ref):
    z, c, x = lax.axis_index(Z), lax.axis_index(C), lax.axis_index(X)
    total = jnp.sum(in_ref[...], axis=0)
    start = (48 * z + 24 * c + 6 * x) & 127
    lane = lax.broadcasted_iota(jnp.int32, (1, F), 1)

    def entry(row, column):
        return jnp.sum(jnp.where(lane == column, total[row : row + 1], 0.0), axis=1, keepdims=True)

    fifth = (start + 4) & 127
    count_head, count_tail = entry(1, start), entry(5, fifth)
    fix_head, fix_tail = entry(0, start + 1), entry(4, fifth + 1)
    sub = lax.broadcasted_iota(jnp.int32, (8, 1), 0)
    wide = lax.broadcasted_iota(jnp.int32, (8, F), 1)
    gram = jnp.where((sub == 1) & (wide == start), fix_head, total)
    gram = jnp.where((sub == 5) & (wide == fifth), fix_tail, gram)
    in_head = start + sub < F
    slot_total = jnp.where(in_head, total[6:7], total[7:8])
    count = jnp.where(in_head, count_head, count_tail)
    own = jnp.sum(jnp.where(wide == ((start + sub) & 127), slot_total, 0.0), axis=1, keepdims=True)
    result = (gram - own * slot_total / count) / (count - 1.0)
    out_ref[...] = result[0:OWN]


def local(features, key_ids, owner):
    packed = pl.pallas_call(
        pack_kernel,
        out_shape=jax.ShapeDtypeStruct((PACK, F), jnp.float32),
        in_specs=[HBM, HBM, HBM],
        out_specs=VMEM,
        scratch_shapes=[
            pltpu.SMEM((KEYS,), jnp.int32),
            pltpu.VMEM((2, F), jnp.int32),
            pltpu.SemaphoreType.DMA((2 + PARTS,)),
        ],
        compiler_params=PARAMS,
        name="pack",
    )(*(pltpu.with_memory_space_constraint(v, pltpu.HBM) for v in (owner, features, key_ids.reshape(2, F))))
    pair = lax.all_gather(packed, (Z, C), axis_index_groups=PAIRS, tiled=True)
    partial = pl.pallas_call(
        gram_kernel,
        out_shape=jax.ShapeDtypeStruct((NY * NX, MSG, F), jnp.float32),
        in_specs=[VMEM],
        out_specs=VMEM,
        compiler_params=PARAMS,
        name="gram",
    )(pair)
    near = lax.all_to_all(partial, (X, Y), 0, 0, axis_index_groups=[NEAR], tiled=True)
    relayed = pl.pallas_call(
        relay_kernel,
        out_shape=jax.ShapeDtypeStruct((8, 8, F), jnp.float32),
        in_specs=[VMEM],
        out_specs=VMEM,
        compiler_params=PARAMS,
        name="relay",
    )(near)
    far = lax.all_to_all(relayed, Z, 0, 0, axis_index_groups=FAR, tiled=True)
    return pl.pallas_call(
        final_kernel,
        out_shape=jax.ShapeDtypeStruct((OWN, F), jnp.float32),
        in_specs=[VMEM],
        out_specs=VMEM,
        compiler_params=PARAMS,
        name="finish",
    )(far)


def solution(mesh):
    torus = Mesh(mesh.devices.reshape(NY, NZ, 2, NX), ALL)
    in_specs = (P(ALL, None), P(ALL), P())
    return jax.shard_map(local, mesh=torus, in_specs=in_specs, out_specs=P(ALL, None), check_vma=False)
```
